32 devices in a mesh: seq: 8 (over z, y), head: 4 (over x, core).
Axes of the slice: x: 2, y: 2, z: 4, core: 2. Of those that a mesh axis runs over, the one named last changes fastest.
Arguments:
- tokens: bfloat16 [4096, 4096], P('seq'), may hold values from -6 to 6
- w_query: bfloat16 [4096, 2048], P('seq', 'head'), may hold values from -0.09375 to 0.09375
- w_key: bfloat16 [4096, 2048], P('seq', 'head'), may hold values from -0.09375 to 0.09375
- w_value: bfloat16 [4096, 2048], P('seq', 'head'), may hold values from -0.09375 to 0.09375
- omega_seed: int32 [16, 128, 256], P('head'), may hold values from -4 to 4
- grad_out: bfloat16 [4096, 2048], P('seq', 'head'), may hold values from -6 to 6
Outputs:
- input_grad: bfloat16 [4096, 4096], P('seq', 'head')
- query_wgrad: float32 [4096, 2048], P('seq', 'head')
- key_wgrad: float32 [4096, 2048], P('seq', 'head')
- value_wgrad: float32 [4096, 2048], P('seq', 'head')
The draws below stay inside these ranges and needn't reach their ends.
Inputs may be any that keep to these rules, and one draw needn't show every extreme that they name: `omega_seed`: the feature seeds are small whole numbers.
All inputs are finite; a program needn't handle non-finite values.
Results may differ from the reference program's by a relative error of at most 0.02.
Values may be sent and summed in bfloat16 or wider, within the bound.
A program may use at most 128 MiB of HBM per device.

```python
import math
import jax
import jax.numpy as jnp
from jax import lax

D = 4096
HD = 128
M = 256
TOK_DEV = 512
HEADS = 16
TOKENS = 4096
N_SEQ = 8


def plant(drawn, rng, smallest, top_value):
    longest = drawn.shape.index(max(drawn.shape))
    spots = []
    for shift in (0, 1):
        where = [jax.random.randint(jax.random.fold_in(rng, axis), (), 0, length) for axis, length in enumerate(drawn.shape)]
        where[longest] = (where[longest] + shift) % drawn.shape[longest]
        spots.append(tuple(where))
    return drawn.at[spots[0]].set(smallest).at[spots[1]].set(top_value)


def steps_of(own_key, dims, shards, low, top_value):
    def one(position, parts):
        steps = jax.random.uniform(jax.random.fold_in(jax.random.fold_in(own_key, 6), position), (parts,), jnp.float32, low / len(shards), top_value / len(shards))
        return jnp.repeat(jnp.exp(steps), dims[position] // parts).reshape((-1,) + (1,) * (len(dims) - position - 1))

    gain = one(*shards[0])
    for cut in shards[1:]:
        gain = gain * one(*cut)
    return gain


def gaussian(rng, dims, scale, limit, shards=(), dtype=jnp.bfloat16):
    array = scale * jax.random.normal(rng, dims, jnp.float32)
    if shards:
        array = array * steps_of(rng, dims, shards, -0.22, 0.18)
    return jnp.clip(array, -limit, limit).astype(dtype)


def setup_inputs(seed: int = 0) -> dict:
    keys = jax.random.split(jax.random.key(seed), 7)
    tokens = gaussian(keys[0], (TOKENS, D), 1.0, 6.0, ((0, 8),))
    w_query = gaussian(keys[1], (D, HEADS * HD), D ** -0.5, 0.09375, ((0, 8), (1, 4)))
    w_key = gaussian(keys[2], (D, HEADS * HD), D ** -0.5, 0.09375, ((0, 8), (1, 4)))
    w_value = gaussian(keys[3], (D, HEADS * HD), D ** -0.5, 0.09375, ((0, 8), (1, 4)))
    omega_seed = plant(jax.random.randint(keys[4], (HEADS, HD, M), -4, 5), jax.random.fold_in(keys[4], 1), -4, 4).astype(jnp.int32)
    grad_out = gaussian(keys[5], (TOKENS, HEADS * HD), 1.0, 6.0, ((0, 8), (1, 4)))
    return {"tokens": tokens, "w_query": w_query, "w_key": w_key, "w_value": w_value, "omega_seed": omega_seed, "grad_out": grad_out}


exact_arithmetic_mode = lax.Precision.HIGHEST
seed_step = 0.4

def feature_map(scaled, projection):
    projected = jnp.einsum('htd,hdm->htm', scaled, projection, precision=exact_arithmetic_mode)
    return jnp.exp(projected - 0.5 * lax.optimization_barrier(jnp.sum(scaled * scaled, -1, keepdims=True))) / math.sqrt(projection.shape[-1])

def feature_grad(upstream, features, scaled, projection):
    weighted = upstream * features
    projected = jnp.einsum('htm,hdm->htd', weighted, projection, precision=exact_arithmetic_mode)
    return (projected - lax.optimization_barrier(jnp.sum(weighted, -1, keepdims=True)) * scaled) * scaled.shape[-1] ** (-0.25)

def blocked(value_matrix):
    return value_matrix.astype(jnp.float32).reshape(N_SEQ, TOK_DEV, HEADS, HD).transpose(0, 2, 1, 3)

def unblocked(value_matrix):
    return value_matrix.transpose(0, 2, 1, 3).reshape(TOKENS, HEADS * HD).astype(jnp.bfloat16)

def back_product(grads, weight):
    return lax.dot_general(grads, weight, (((1,), (1,)), ((), ())), preferred_element_type=jnp.float32)

def reference(tokens, w_query, w_key, w_value, omega_seed, grad_out):
    query_act = jnp.dot(tokens, w_query, preferred_element_type=jnp.float32).astype(jnp.bfloat16)
    key_act = jnp.dot(tokens, w_key, preferred_element_type=jnp.float32).astype(jnp.bfloat16)
    value_act = jnp.dot(tokens, w_value, preferred_element_type=jnp.float32).astype(jnp.bfloat16)
    projection = omega_seed.astype(jnp.float32) * seed_step
    scale_in = HD ** (-0.25)
    query_scaled = blocked(query_act) * scale_in
    key_scaled = blocked(key_act) * scale_in
    value_matrix = blocked(value_act)
    upstream = blocked(grad_out)
    causal = jnp.tril(jnp.ones((TOK_DEV, TOK_DEV), jnp.float32))

    def forward_block(carry, inputs):
        prefix_carried_outer, prefix_normaliser_accrual = carry
        q_scaled, k_scaled, value_block_rows, grad_rows = inputs
        query_feature_rows = feature_map(q_scaled, projection)
        source_embedding_entries = feature_map(k_scaled, projection)
        attention_scores = jnp.einsum('htm,hsm->hts', query_feature_rows, source_embedding_entries, precision=exact_arithmetic_mode) * causal
        attention_numerator = jnp.einsum('xyw,xwc->xyc', attention_scores, value_block_rows, precision=exact_arithmetic_mode) + jnp.einsum('sji,six->sjx', query_feature_rows, prefix_carried_outer, precision=exact_arithmetic_mode)
        normer = lax.optimization_barrier(jnp.sum(attention_scores, -1)) + jnp.einsum('htm,hm->ht', query_feature_rows, prefix_normaliser_accrual, precision=exact_arithmetic_mode)
        output = attention_numerator / normer[..., None]
        dividend_cotangent = grad_rows / normer[..., None]
        normaliser_cotangent = -lax.optimization_barrier(jnp.sum(grad_rows * output, -1)) / normer
        couplewise_products = (jnp.einsum('htd,hsd->hts', dividend_cotangent, value_block_rows, precision=exact_arithmetic_mode) + normaliser_cotangent[..., None]) * causal
        target_embedding_cotangent = jnp.einsum('mez,mzo->meo', couplewise_products, source_embedding_entries, precision=exact_arithmetic_mode) + jnp.einsum('zrc,zfc->zrf', dividend_cotangent, prefix_carried_outer, precision=exact_arithmetic_mode) + normaliser_cotangent[..., None] * prefix_normaliser_accrual[:, None, :]
        query_grad = feature_grad(target_embedding_cotangent, query_feature_rows, q_scaled, projection)
        updated_states = prefix_carried_outer + jnp.einsum('vzn,vza->vna', source_embedding_entries, value_block_rows, precision=exact_arithmetic_mode)
        new_totals = prefix_normaliser_accrual + lax.optimization_barrier(jnp.sum(source_embedding_entries, 1))
        return ((updated_states, new_totals), (query_grad, dividend_cotangent, normaliser_cotangent))
    start_states = jnp.zeros((HEADS, M, HD), jnp.float32)
    start_totals = jnp.zeros((HEADS, M), jnp.float32)
    carried, results = lax.scan(forward_block, (start_states, start_totals), (query_scaled, key_scaled, value_matrix, upstream))
    query_grad, dividend_cotangent, normaliser_cotangent = results

    def backward_block(carry, inputs):
        subsequent_states, subsequent_sum = carry
        q_scaled, k_scaled, value_block_rows, numerator_rows, den_rows = inputs
        query_feature_rows = feature_map(q_scaled, projection)
        source_embedding_entries = feature_map(k_scaled, projection)
        attention_scores = jnp.einsum('htm,hsm->hts', query_feature_rows, source_embedding_entries, precision=exact_arithmetic_mode) * causal
        couplewise_products = (jnp.einsum('htd,hsd->hts', numerator_rows, value_block_rows, precision=exact_arithmetic_mode) + den_rows[..., None]) * causal
        key_feature_gradient = jnp.einsum('ykl,yku->ylu', couplewise_products, query_feature_rows, precision=exact_arithmetic_mode) + jnp.einsum('bgq,bxq->bgx', value_block_rows, subsequent_states, precision=exact_arithmetic_mode) + subsequent_sum[:, None, :]
        value_gradient_rows = jnp.einsum('vkm,vky->vmy', attention_scores, numerator_rows, precision=exact_arithmetic_mode) + jnp.einsum('tjr,tro->tjo', source_embedding_entries, subsequent_states, precision=exact_arithmetic_mode)
        key_grad = feature_grad(key_feature_gradient, source_embedding_entries, k_scaled, projection)
        updated_states = subsequent_states + jnp.einsum('opu,opc->ouc', query_feature_rows, numerator_rows, precision=exact_arithmetic_mode)
        new_sum = subsequent_sum + jnp.einsum('htm,ht->hm', query_feature_rows, den_rows, precision=exact_arithmetic_mode)
        return ((updated_states, new_sum), (key_grad, value_gradient_rows))
    carried_back, results_back = lax.scan(backward_block, (start_states, start_totals), (query_scaled, key_scaled, value_matrix, dividend_cotangent, normaliser_cotangent), reverse=True)
    key_grad, value_gradient_rows = results_back
    query16 = unblocked(query_grad)
    key16 = unblocked(key_grad)
    value16 = unblocked(value_gradient_rows)
    input_grad = (back_product(query16, w_query) + back_product(key16, w_key) + back_product(value16, w_value)).astype(jnp.bfloat16)
    joined = jnp.concatenate([query16, key16, value16], 1)
    token_blocks = tokens.reshape(N_SEQ, TOK_DEV, D)
    grad_blocks = joined.reshape(N_SEQ, TOK_DEV, 3 * HEADS * HD)

    def weight_block(total, pieces):
        token_rows, grad_rows = pieces
        partial_value = lax.dot_general(token_rows, grad_rows, (((0,), (0,)), ((), ())), preferred_element_type=jnp.float32)
        partial_value = lax.optimization_barrier(partial_value.astype(jnp.bfloat16)).astype(jnp.float32)
        return (total + partial_value, None)
    start_total = jnp.zeros((D, 3 * HEADS * HD), jnp.float32)
    weight_total, unused = lax.scan(weight_block, start_total, (token_blocks, grad_blocks))
    columns = HEADS * HD
    return (input_grad, weight_total[:, :columns], weight_total[:, columns:2 * columns], weight_total[:, 2 * columns:])
```

```python
import functools
import math

import jax
import jax.numpy as jnp
from jax import lax
from jax.experimental import pallas as pl
from jax.experimental.pallas import tpu as pltpu
from jax.sharding import PartitionSpec as P

seed_step = 0.4
MESH = pl.DeviceIdType.MESH
VMEM = pl.BlockSpec(memory_space=pltpu.VMEM)


def ein(spec, a, b):
    return jnp.einsum(
        spec,
        a.astype(jnp.bfloat16),
        b.astype(jnp.bfloat16),
        preferred_element_type=jnp.float32,
    )


def ring_index(pos, n):
    pos = lax.rem(pos + 2 * n, n)
    odd = lax.div(pos, n // 2)
    return (1 - odd) * (2 * pos) + odd * (2 * (n - 1 - pos) + 1)


def ring_pos(index, n):
    odd = lax.rem(index, 2)
    half = lax.div(index, 2)
    return (1 - odd) * half + odd * (n - 1 - half)


def greet_ring(ahead, behind, others):
    barrier = pltpu.get_barrier_semaphore()
    for device in ({"seq": ahead}, {"seq": behind}):
        pl.semaphore_signal(barrier, inc=1, device_id=device, device_id_type=MESH)
    for device in others:
        pl.semaphore_signal(barrier, inc=1, device_id=device, device_id_type=MESH)
    pl.semaphore_wait(barrier, 2 + len(others))


def project_kernel(n, tok_ref, w_ref, act_ref, full_ref, acc, local_sem, send_sem, recv_sem):
    me = lax.axis_index("seq")
    place = ring_pos(me, n)
    ahead, behind = ring_index(place + 1, n), ring_index(place - 1, n)
    rows = w_ref.shape[1]
    greet_ring(ahead, behind, ())
    own = pltpu.make_async_copy(w_ref, full_ref.at[:, me], local_sem)
    own.start()
    acc[...] = jnp.zeros_like(acc)
    own.wait()

    def owner_of(way, step):
        return ring_index(place - step if way == 0 else place + step, n)

    def multiply(step):
        for way in range(2):
            owner = owner_of(way, step)
            columns = pl.ds(pl.multiple_of(owner * rows, rows), rows)
            acc[way] += jnp.dot(
                tok_ref[:, columns], full_ref[way, owner], preferred_element_type=jnp.float32
            )

    def one(step, carry):
        copies = []
        for way, target in ((0, ahead), (1, behind)):
            owner = owner_of(way, step)
            copies.append(
                pltpu.make_async_remote_copy(
                    src_ref=full_ref.at[way, owner],
                    dst_ref=full_ref.at[way, owner],
                    send_sem=send_sem.at[way, step],
                    recv_sem=recv_sem.at[way, step],
                    device_id={"seq": target},
                    device_id_type=MESH,
                )
            )
        for copy in copies:
            copy.start()
        multiply(step)
        for copy in copies:
            copy.wait()
        return carry

    lax.fori_loop(0, n - 1, one, 0)
    multiply(n - 1)
    act_ref[...] = acc[...].astype(act_ref.dtype)


def project(tokens, weights, n):
    ways, rows, width = weights.shape
    toks = tokens.shape[0]
    return pl.pallas_call(
        functools.partial(project_kernel, n),
        out_shape=(
            jax.ShapeDtypeStruct((ways, toks, width), jnp.bfloat16),
            jax.ShapeDtypeStruct((ways, n, rows, width), jnp.bfloat16),
        ),
        in_specs=[VMEM, VMEM],
        out_specs=(VMEM, VMEM),
        scratch_shapes=[
            pltpu.VMEM((ways, toks, width), jnp.float32),
            pltpu.SemaphoreType.DMA,
            pltpu.SemaphoreType.DMA((2, n - 1)),
            pltpu.SemaphoreType.DMA((2, n - 1)),
        ],
        compiler_params=pltpu.CompilerParams(
            collective_id=0, has_side_effects=True, vmem_limit_bytes=56 << 20
        ),
        cost_estimate=pl.CostEstimate(
            flops=2 * toks * n * rows * ways * width, bytes_accessed=1 << 24, transcendentals=0
        ),
    )(tokens, weights)


def scan_kernel(n, sign, x_ref, out_ref, total, send_buf, recv_buf, send_sem, recv_sem):
    me = lax.axis_index("seq")
    steps = [1 << b for b in range((n - 1).bit_length())]
    barrier = pltpu.get_barrier_semaphore()
    for far in steps:
        source = lax.rem(me - sign * far + n, n)
        pl.semaphore_signal(barrier, inc=1, device_id={"seq": source}, device_id_type=MESH)
    pl.semaphore_wait(barrier, len(steps))
    total[...] = x_ref[...]
    out_ref[...] = jnp.zeros_like(out_ref)
    rank = me if sign == 1 else n - 1 - me
    for place, far in enumerate(steps):
        send_buf[place] = total[...].astype(jnp.bfloat16)
        copy = pltpu.make_async_remote_copy(
            src_ref=send_buf.at[place],
            dst_ref=recv_buf.at[place],
            send_sem=send_sem.at[place],
            recv_sem=recv_sem.at[place],
            device_id={"seq": lax.rem(me + sign * far + n, n)},
            device_id_type=MESH,
        )
        copy.start()
        copy.wait()
        keep = jnp.broadcast_to(rank >= far, out_ref.shape)
        got = jnp.where(keep, recv_buf[place].astype(jnp.float32), 0.0)
        total[...] += got
        out_ref[...] += got


def carried(states, totals, n, sign):
    heads, features, size = states.shape
    flat_totals = totals.reshape(-1, size)
    used = flat_totals.shape[0]
    pad = (-(used)) % 16
    packed = jnp.concatenate(
        [states.reshape(-1, size), flat_totals, jnp.zeros((pad, size), jnp.float32)], 0
    )
    steps = (n - 1).bit_length()
    out = pl.pallas_call(
        functools.partial(scan_kernel, n, sign),
        out_shape=jax.ShapeDtypeStruct(packed.shape, jnp.float32),
        in_specs=[VMEM],
        out_specs=VMEM,
        scratch_shapes=[
            pltpu.VMEM(packed.shape, jnp.float32),
            pltpu.VMEM((steps,) + packed.shape, jnp.bfloat16),
            pltpu.VMEM((steps,) + packed.shape, jnp.bfloat16),
            pltpu.SemaphoreType.DMA((steps,)),
            pltpu.SemaphoreType.DMA((steps,)),
        ],
        compiler_params=pltpu.CompilerParams(
            collective_id=1 if sign == 1 else 2,
            has_side_effects=True,
            vmem_limit_bytes=32 << 20,
        ),
    )(packed)
    split = heads * features
    return out[:split].reshape(states.shape), out[split : split + used].reshape(totals.shape)


def grads_kernel(
    n, groups, tok_ref, grad_ref, full_ref, input_ref, weight_ref,
    ring, part_out, part_in, send_sem, recv_sem, part_send, part_recv,
):
    me = lax.axis_index("seq")
    group = lax.axis_index("head")
    place = ring_pos(me, n)
    ahead, behind = ring_index(place + 1, n), ring_index(place - 1, n)
    rows = full_ref.shape[2]
    others = tuple({"head": lax.rem(group + k, groups)} for k in range(1, groups))
    greet_ring(ahead, behind, others)

    def term(way, step):
        owner = ring_index(place - 1 - step if way == 0 else place + 1 + step, n)
        columns = pl.ds(pl.multiple_of(owner * rows, rows), rows)
        return lax.dot_general(
            tok_ref[:, columns],
            grad_ref[way],
            (((0,), (0,)), ((), ())),
            preferred_element_type=jnp.float32,
        )

    def ring_copy(way, step):
        return pltpu.make_async_remote_copy(
            src_ref=ring.at[way, step],
            dst_ref=ring.at[way, step + 1],
            send_sem=send_sem.at[way, step],
            recv_sem=recv_sem.at[way, step],
            device_id={"seq": ahead if way == 0 else behind},
            device_id_type=MESH,
        )

    for way in range(2):
        ring[way, 0] = term(way, 0).astype(jnp.bfloat16)
        ring_copy(way, 0).start()

    def part_copy(k):
        return pltpu.make_async_remote_copy(
            src_ref=part_out.at[k],
            dst_ref=part_in.at[k],
            send_sem=part_send.at[k],
            recv_sem=part_recv.at[k],
            device_id={"head": lax.rem(group + k + 1, groups)},
            device_id_type=MESH,
        )

    blocks = n // groups

    def one_part(k, carry):
        first = lax.rem(group + k + 1, groups) * blocks

        def one_block(c, carry):
            piece = None
            for way in range(2):
                product = lax.dot_general(
                    grad_ref[way],
                    full_ref[way, first + c],
                    (((1,), (1,)), ((), ())),
                    preferred_element_type=jnp.float32,
                )
                piece = product if piece is None else piece + product
            columns = pl.ds(pl.multiple_of(c * rows, rows), rows)
            part_out[k, :, columns] = piece.astype(jnp.bfloat16)
            return carry

        lax.fori_loop(0, blocks, one_block, 0)

        @pl.when(k < groups - 1)
        def _():
            part_copy(k).start()

        return carry

    lax.fori_loop(0, groups, one_part, 0)

    def one(step, carry):
        for way in range(2):
            own = term(way, step)
            ring_copy(way, step - 1).wait()
            ring[way, step] = (ring[way, step].astype(jnp.float32) + own).astype(jnp.bfloat16)
            ring_copy(way, step).start()
        return carry

    lax.fori_loop(1, n - 1, one, 0)
    total = part_out[groups - 1].astype(jnp.float32)
    for k in range(groups - 1):
        part_copy(k).wait()
        total += part_in[k].astype(jnp.float32)
    input_ref[...] = total.astype(input_ref.dtype)
    for way in range(2):
        own = term(way, n - 1)
        ring_copy(way, n - 2).wait()
        weight_ref[way] = ring[way, n - 1].astype(jnp.float32) + own


def gradients(tokens, grads, full, n, groups):
    ways, _, rows, width = full.shape
    toks, model = tokens.shape
    share = model // groups
    return pl.pallas_call(
        functools.partial(grads_kernel, n, groups),
        out_shape=(
            jax.ShapeDtypeStruct((toks, share), jnp.bfloat16),
            jax.ShapeDtypeStruct((ways, rows, width), jnp.float32),
        ),
        in_specs=[VMEM, VMEM, VMEM],
        out_specs=(VMEM, VMEM),
        scratch_shapes=[
            pltpu.VMEM((ways, n, rows, width), jnp.bfloat16),
            pltpu.VMEM((groups, toks, share), jnp.bfloat16),
            pltpu.VMEM((groups - 1, toks, share), jnp.bfloat16),
            pltpu.SemaphoreType.DMA((2, n - 1)),
            pltpu.SemaphoreType.DMA((2, n - 1)),
            pltpu.SemaphoreType.DMA((groups - 1,)),
            pltpu.SemaphoreType.DMA((groups - 1,)),
        ],
        compiler_params=pltpu.CompilerParams(
            collective_id=3, has_side_effects=True, vmem_limit_bytes=58 << 20
        ),
    )(tokens, grads, full)


def two_ways(a):
    return a.reshape(a.shape[0], 2, -1).transpose(1, 0, 2)


def feature_map(act, seed, scaled):
    factor = seed_step * act.shape[-1] ** (-0.25)
    projected = ein("htd,hdm->htm", act, seed) * factor
    return jnp.exp(projected - 0.5 * jnp.sum(scaled * scaled, -1, keepdims=True)) / math.sqrt(
        seed.shape[-1]
    )


def feature_grad(upstream, features, scaled, seed):
    weighted = upstream * features
    projected = ein("htm,hdm->htd", weighted, seed) * seed_step
    return (projected - jnp.sum(weighted, -1, keepdims=True) * scaled) * scaled.shape[-1] ** (-0.25)


def head_major(value_matrix, heads_here):
    tok_rows = value_matrix.shape[0]
    return value_matrix.astype(jnp.float32).reshape(tok_rows, heads_here, -1).transpose(1, 0, 2)


def token_major(value_matrix):
    return value_matrix.transpose(1, 0, 2).reshape(value_matrix.shape[1], -1).astype(jnp.bfloat16)


def per_device(n, groups, tokens, w_query, w_key, w_value, omega_seed, grad_out):
    heads_here = omega_seed.shape[0]
    head_size = omega_seed.shape[1]
    weights = two_ways(jnp.concatenate([w_query, w_key, w_value], 1))
    activations, full = project(tokens, weights, n)
    both = activations.transpose(1, 0, 2).reshape(tokens.shape[0], -1)
    query_act, key_act, value_act = jnp.split(both, 3, 1)
    scale_in = head_size ** (-0.25)
    query_rows = head_major(query_act, heads_here)
    query_scaled = query_rows * scale_in
    key_rows = head_major(key_act, heads_here)
    key_scaled = key_rows * scale_in
    value_matrix = head_major(value_act, heads_here)
    upstream = head_major(grad_out, heads_here)
    query_feature_rows = feature_map(query_rows, omega_seed, query_scaled)
    source_embedding_entries = feature_map(key_rows, omega_seed, key_scaled)
    tok_rows = tokens.shape[0]
    causal = jnp.tril(jnp.ones((tok_rows, tok_rows), jnp.float32))
    block_local_states = ein(
        "vzn,vza->vna", source_embedding_entries, value_matrix
    )
    local_totals = jnp.sum(source_embedding_entries, 1)
    prefix_carried_outer, prefix_normaliser_accrual = carried(
        block_local_states, local_totals, n, 1
    )
    attention_scores = (
        ein(
            "htm,hsm->hts",
            query_feature_rows,
            source_embedding_entries
        )
        * causal
    )
    attention_numerator = ein(
        "xyw,xwc->xyc", attention_scores, value_matrix
    ) + ein(
        "sji,six->sjx", query_feature_rows, prefix_carried_outer
    )
    normer = jnp.sum(attention_scores, -1) + ein(
        "htm,hm->ht", query_feature_rows, prefix_normaliser_accrual
    )
    output = attention_numerator / normer[..., None]
    dividend_cotangent = upstream / normer[..., None]
    normaliser_cotangent = -jnp.sum(upstream * output, -1) / normer
    couplewise_products = (
        ein(
            "htd,hsd->hts", dividend_cotangent, value_matrix
        )
        + normaliser_cotangent[..., None]
    ) * causal
    target_embedding_cotangent = (
        ein(
            "mez,mzo->meo",
            couplewise_products,
            source_embedding_entries
        )
        + ein(
            "zrc,zfc->zrf",
            dividend_cotangent,
            prefix_carried_outer
        )
        + normaliser_cotangent[..., None] * prefix_normaliser_accrual[:, None, :]
    )
    query16 = token_major(
        feature_grad(target_embedding_cotangent, query_feature_rows, query_scaled, omega_seed)
    )
    subsequent_local_states = ein(
        "opu,opc->ouc", query_feature_rows, dividend_cotangent
    )
    later_totals = ein(
        "htm,ht->hm", query_feature_rows, normaliser_cotangent
    )
    subsequent_states, subsequent_sum = carried(
        subsequent_local_states, later_totals, n, -1
    )
    key_feature_gradient = (
        ein(
            "ykl,yku->ylu", couplewise_products, query_feature_rows
        )
        + ein(
            "bgq,bxq->bgx", value_matrix, subsequent_states
        )
        + subsequent_sum[:, None, :]
    )
    value_gradient_rows = ein(
        "vkm,vky->vmy", attention_scores, dividend_cotangent
    ) + ein(
        "tjr,tro->tjo", source_embedding_entries, subsequent_states
    )
    key16 = token_major(
        feature_grad(key_feature_gradient, source_embedding_entries, key_scaled, omega_seed)
    )
    value16 = token_major(value_gradient_rows)
    joined = jnp.concatenate([query16, key16, value16], 1)
    input_grad, weight_total = gradients(tokens, two_ways(joined), full, n, groups)
    weight_total = weight_total.transpose(1, 0, 2).reshape(w_query.shape[0], -1)
    columns = query16.shape[1]
    query_wgrad = weight_total[:, :columns]
    key_wgrad = weight_total[:, columns : 2 * columns]
    value_wgrad = weight_total[:, 2 * columns :]
    return (input_grad, query_wgrad, key_wgrad, value_wgrad)


def solution(mesh):
    placed = (
        P("seq", None),
        P("seq", "head"),
        P("seq", "head"),
        P("seq", "head"),
        P("head", None, None),
        P("seq", "head"),
    )
    return jax.shard_map(
        functools.partial(per_device, mesh.shape["seq"], mesh.shape["head"]),
        mesh=mesh,
        in_specs=placed,
        out_specs=(P("seq", "head"), P("seq", "head"), P("seq", "head"), P("seq", "head")),
        check_vma=False,
    )
```

```python
import functools
import math

import jax
import jax.numpy as jnp
from jax import lax
from jax.experimental import pallas as pl
from jax.experimental.pallas import tpu as pltpu
from jax.sharding import PartitionSpec as P

seed_step = 0.4
MESH = pl.DeviceIdType.MESH
VMEM = pl.BlockSpec(memory_space=pltpu.VMEM)


def ein(spec, a, b):
    return jnp.einsum(
        spec,
        a.astype(jnp.bfloat16),
        b.astype(jnp.bfloat16),
        preferred_element_type=jnp.float32,
    )


def ring_index(pos, n):
    pos = lax.rem(pos + 2 * n, n)
    odd = lax.div(pos, n // 2)
    return (1 - odd) * (2 * pos) + odd * (2 * (n - 1 - pos) + 1)


def ring_pos(index, n):
    odd = lax.rem(index, 2)
    half = lax.div(index, 2)
    return (1 - odd) * half + odd * (n - 1 - half)


def greet_ring(ahead, behind, others):
    barrier = pltpu.get_barrier_semaphore()
    for device in ({"seq": ahead}, {"seq": behind}):
        pl.semaphore_signal(barrier, inc=1, device_id=device, device_id_type=MESH)
    for device in others:
        pl.semaphore_signal(barrier, inc=1, device_id=device, device_id_type=MESH)
    pl.semaphore_wait(barrier, 2 + len(others))


def pieces_of(rows):
    half = rows // 2
    return tuple((part, pl.ds(part * half, half)) for part in range(2))


def split_columns(cols):
    half = cols // 2
    return (
        (0, slice(0, cols), 0, slice(0, cols)),
        (1, slice(0, half), 0, slice(cols, cols + half)),
        (1, slice(half, cols), 1, slice(0, half)),
        (2, slice(0, cols), 1, slice(half, half + cols)),
    )


def project_kernel(
    n, tok_ref, wq_ref, wk_ref, wv_ref, q_ref, k_ref, v_ref, full_ref, acc, send_sem, recv_sem
):
    me = lax.axis_index("seq")
    place = ring_pos(me, n)
    ahead, behind = ring_index(place + 1, n), ring_index(place - 1, n)
    rows, cols = wq_ref.shape
    greet_ring(ahead, behind, ())
    sources = (wq_ref, wk_ref, wv_ref)
    for matrix, columns, way, target in split_columns(cols):
        full_ref[way, me, :, target] = sources[matrix][:, columns]

    def owner_of(way, step):
        return ring_index(place - step if way == 0 else place + step, n)

    def ring_copy(way, step, part, span):
        owner = owner_of(way, step)
        return pltpu.make_async_remote_copy(
            src_ref=full_ref.at[way, owner, span],
            dst_ref=full_ref.at[way, owner, span],
            send_sem=send_sem.at[way, step, part],
            recv_sem=recv_sem.at[way, step, part],
            device_id={"seq": ahead if way == 0 else behind},
            device_id_type=MESH,
        )

    def arrival(way, step, part, span):
        owner = owner_of(way, step + 1)
        return pltpu.make_async_remote_copy(
            src_ref=full_ref.at[way, owner, span],
            dst_ref=full_ref.at[way, owner, span],
            send_sem=send_sem.at[way, step, part],
            recv_sem=recv_sem.at[way, step, part],
            device_id={"seq": ahead if way == 0 else behind},
            device_id_type=MESH,
        )

    def multiply(step):
        for way in range(2):
            owner = owner_of(way, step)
            columns = pl.ds(pl.multiple_of(owner * rows, rows), rows)
            acc[way] += jnp.dot(
                tok_ref[:, columns], full_ref[way, owner], preferred_element_type=jnp.float32
            )

    for part, span in pieces_of(rows):
        for way in range(2):
            ring_copy(way, 0, part, span).start()
    acc[...] = jnp.zeros_like(acc)
    multiply(0)

    def one(step, carry):
        for part, span in pieces_of(rows):
            for way in range(2):
                arrival(way, step - 1, part, span).wait_recv()
                ring_copy(way, step, part, span).start()
        multiply(step)
        return carry

    lax.fori_loop(1, n - 1, one, 0)
    for part, span in pieces_of(rows):
        for way in range(2):
            arrival(way, n - 2, part, span).wait_recv()
    multiply(n - 1)
    results = (q_ref, k_ref, v_ref)
    for matrix, columns, way, source in split_columns(cols):
        results[matrix][:, columns] = acc[way, :, source].astype(jnp.bfloat16)

    def sent(step, carry):
        for part, span in pieces_of(rows):
            for way in range(2):
                ring_copy(way, step, part, span).wait_send()
        return carry

    lax.fori_loop(0, n - 1, sent, 0)


def project(tokens, w_query, w_key, w_value, n):
    rows, cols = w_query.shape
    width = 3 * cols // 2
    toks = tokens.shape[0]
    act = jax.ShapeDtypeStruct((toks, cols), jnp.bfloat16)
    return pl.pallas_call(
        functools.partial(project_kernel, n),
        out_shape=(act, act, act, jax.ShapeDtypeStruct((2, n, rows, width), jnp.bfloat16)),
        in_specs=[VMEM] * 4,
        out_specs=(VMEM,) * 4,
        scratch_shapes=[
            pltpu.VMEM((2, toks, width), jnp.float32),
            pltpu.SemaphoreType.DMA((2, n - 1, 2)),
            pltpu.SemaphoreType.DMA((2, n - 1, 2)),
        ],
        compiler_params=pltpu.CompilerParams(
            collective_id=0, has_side_effects=True, vmem_limit_bytes=56 << 20
        ),
        cost_estimate=pl.CostEstimate(
            flops=4 * toks * n * rows * width, bytes_accessed=1 << 24, transcendentals=0
        ),
    )(tokens, w_query, w_key, w_value)


def scan_kernel(n, sign, x_ref, out_ref, total, send_buf, recv_buf, send_sem, recv_sem):
    me = lax.axis_index("seq")
    steps = [1 << b for b in range((n - 1).bit_length())]
    barrier = pltpu.get_barrier_semaphore()
    for far in steps:
        source = lax.rem(me - sign * far + n, n)
        pl.semaphore_signal(barrier, inc=1, device_id={"seq": source}, device_id_type=MESH)
    pl.semaphore_wait(barrier, len(steps))
    total[...] = x_ref[...]
    out_ref[...] = jnp.zeros_like(out_ref)
    rank = me if sign == 1 else n - 1 - me
    for place, far in enumerate(steps):
        send_buf[place] = total[...].astype(jnp.bfloat16)
        copy = pltpu.make_async_remote_copy(
            src_ref=send_buf.at[place],
            dst_ref=recv_buf.at[place],
            send_sem=send_sem.at[place],
            recv_sem=recv_sem.at[place],
            device_id={"seq": lax.rem(me + sign * far + n, n)},
            device_id_type=MESH,
        )
        copy.start()
        copy.wait()
        keep = jnp.broadcast_to(rank >= far, out_ref.shape)
        got = jnp.where(keep, recv_buf[place].astype(jnp.float32), 0.0)
        total[...] += got
        out_ref[...] += got


def carried(states, totals, n, sign):
    heads, features, size = states.shape
    flat_totals = totals.reshape(-1, size)
    used = flat_totals.shape[0]
    pad = (-(used)) % 16
    packed = jnp.concatenate(
        [states.reshape(-1, size), flat_totals, jnp.zeros((pad, size), jnp.float32)], 0
    )
    steps = (n - 1).bit_length()
    out = pl.pallas_call(
        functools.partial(scan_kernel, n, sign),
        out_shape=jax.ShapeDtypeStruct(packed.shape, jnp.float32),
        in_specs=[VMEM],
        out_specs=VMEM,
        scratch_shapes=[
            pltpu.VMEM(packed.shape, jnp.float32),
            pltpu.VMEM((steps,) + packed.shape, jnp.bfloat16),
            pltpu.VMEM((steps,) + packed.shape, jnp.bfloat16),
            pltpu.SemaphoreType.DMA((steps,)),
            pltpu.SemaphoreType.DMA((steps,)),
        ],
        compiler_params=pltpu.CompilerParams(
            collective_id=1 if sign == 1 else 2,
            has_side_effects=True,
            vmem_limit_bytes=32 << 20,
        ),
    )(packed)
    split = heads * features
    return out[:split].reshape(states.shape), out[split : split + used].reshape(totals.shape)


def grads_kernel(
    n, groups, tok_ref, q_ref, k_ref, v_ref, full_ref, input_ref, wq_ref, wk_ref, wv_ref,
    grad_ref, ring, own, part_out, part_in, send_sem, recv_sem, part_send, part_recv,
):
    me = lax.axis_index("seq")
    group = lax.axis_index("head")
    place = ring_pos(me, n)
    ahead, behind = ring_index(place + 1, n), ring_index(place - 1, n)
    rows = full_ref.shape[2]
    cols = q_ref.shape[1]
    others = tuple({"head": lax.rem(group + k, groups)} for k in range(1, groups))
    greet_ring(ahead, behind, others)
    sources = (q_ref, k_ref, v_ref)
    for matrix, columns, way, target in split_columns(cols):
        grad_ref[way, :, target] = sources[matrix][:, columns]

    def term(way, step):
        owner = ring_index(place - 1 - step if way == 0 else place + 1 + step, n)
        columns = pl.ds(pl.multiple_of(owner * rows, rows), rows)
        own[way] = lax.dot_general(
            tok_ref[:, columns],
            grad_ref[way],
            (((0,), (0,)), ((), ())),
            preferred_element_type=jnp.float32,
        )

    def ring_copy(way, step, part, span):
        return pltpu.make_async_remote_copy(
            src_ref=ring.at[way, step, span],
            dst_ref=ring.at[way, step + 1, span],
            send_sem=send_sem.at[way, step, part],
            recv_sem=recv_sem.at[way, step, part],
            device_id={"seq": ahead if way == 0 else behind},
            device_id_type=MESH,
        )

    def part_copy(k):
        return pltpu.make_async_remote_copy(
            src_ref=part_out.at[k],
            dst_ref=part_in.at[k],
            send_sem=part_send.at[k],
            recv_sem=part_recv.at[k],
            device_id={"head": lax.rem(group + k + 1, groups)},
            device_id_type=MESH,
        )

    blocks = n // groups

    def one_part(k, carry):
        first = lax.rem(group + k + 1, groups) * blocks

        def one_block(c, carry):
            piece = None
            for way in range(2):
                product = lax.dot_general(
                    grad_ref[way],
                    full_ref[way, first + c],
                    (((1,), (1,)), ((), ())),
                    preferred_element_type=jnp.float32,
                )
                piece = product if piece is None else piece + product
            columns = pl.ds(pl.multiple_of(c * rows, rows), rows)
            part_out[k, :, columns] = piece.astype(jnp.bfloat16)
            return carry

        lax.fori_loop(0, blocks, one_block, 0)

        @pl.when(k < groups - 1)
        def _():
            part_copy(k).start()

        return carry

    for way in range(2):
        term(way, 0)
        for part, span in pieces_of(rows):
            ring[way, 0, span] = own[way, span].astype(jnp.bfloat16)
            ring_copy(way, 0, part, span).start()
    for way in range(2):
        term(way, 1)

    def one(step, carry):
        @pl.when(step <= groups)
        def _():
            one_part(step - 1, 0)

        for part, span in pieces_of(rows):
            for way in range(2):
                ring_copy(way, step - 1, part, span).wait_recv()
                ring[way, step, span] = (
                    ring[way, step, span].astype(jnp.float32) + own[way, span]
                ).astype(jnp.bfloat16)
                ring_copy(way, step, part, span).start()
        for way in range(2):
            term(way, step + 1)
        return carry

    lax.fori_loop(1, n - 1, one, 0)
    if groups > n - 2:
        lax.fori_loop(n - 2, groups, one_part, 0)
    total = part_out[groups - 1].astype(jnp.float32)
    for k in range(groups - 1):
        part_copy(k).wait()
        total += part_in[k].astype(jnp.float32)
    input_ref[...] = total.astype(input_ref.dtype)
    for part, span in pieces_of(rows):
        for way in range(2):
            ring_copy(way, n - 2, part, span).wait_recv()
    results = (wq_ref, wk_ref, wv_ref)
    for matrix, columns, way, source in split_columns(cols):
        results[matrix][:, columns] = (
            ring[way, n - 1, :, source].astype(jnp.float32) + own[way, :, source]
        )

    def sent(step, carry):
        for part, span in pieces_of(rows):
            for way in range(2):
                ring_copy(way, step, part, span).wait_send()
        return carry

    lax.fori_loop(0, n - 1, sent, 0)


def gradients(tokens, query16, key16, value16, full, n, groups):
    ways, _, rows, width = full.shape
    toks, model = tokens.shape
    share = model // groups
    wgrad = jax.ShapeDtypeStruct((rows, query16.shape[1]), jnp.float32)
    return pl.pallas_call(
        functools.partial(grads_kernel, n, groups),
        out_shape=(jax.ShapeDtypeStruct((toks, share), jnp.bfloat16), wgrad, wgrad, wgrad),
        in_specs=[VMEM] * 5,
        out_specs=(VMEM,) * 4,
        scratch_shapes=[
            pltpu.VMEM((ways, toks, width), jnp.bfloat16),
            pltpu.VMEM((ways, n, rows, width), jnp.bfloat16),
            pltpu.VMEM((ways, rows, width), jnp.float32),
            pltpu.VMEM((groups, toks, share), jnp.bfloat16),
            pltpu.VMEM((groups - 1, toks, share), jnp.bfloat16),
            pltpu.SemaphoreType.DMA((2, n - 1, 2)),
            pltpu.SemaphoreType.DMA((2, n - 1, 2)),
            pltpu.SemaphoreType.DMA((groups - 1,)),
            pltpu.SemaphoreType.DMA((groups - 1,)),
        ],
        compiler_params=pltpu.CompilerParams(
            collective_id=3, has_side_effects=True, vmem_limit_bytes=60 << 20
        ),
    )(tokens, query16, key16, value16, full)


def feature_map(act, seed, scaled):
    factor = seed_step * act.shape[-1] ** (-0.25)
    projected = ein("htd,hdm->htm", act, seed) * factor
    return jnp.exp(projected - 0.5 * jnp.sum(scaled * scaled, -1, keepdims=True)) / math.sqrt(
        seed.shape[-1]
    )


def feature_grad(upstream, features, scaled, seed):
    weighted = upstream * features
    projected = ein("htm,hdm->htd", weighted, seed) * seed_step
    return (projected - jnp.sum(weighted, -1, keepdims=True) * scaled) * scaled.shape[-1] ** (-0.25)


def head_major(value_matrix, heads_here):
    tok_rows = value_matrix.shape[0]
    return value_matrix.astype(jnp.float32).reshape(tok_rows, heads_here, -1).transpose(1, 0, 2)


def token_major(value_matrix):
    return value_matrix.transpose(1, 0, 2).reshape(value_matrix.shape[1], -1).astype(jnp.bfloat16)


def per_device(n, groups, tokens, w_query, w_key, w_value, omega_seed, grad_out):
    heads_here = omega_seed.shape[0]
    head_size = omega_seed.shape[1]
    query_act, key_act, value_act, full = project(tokens, w_query, w_key, w_value, n)
    scale_in = head_size ** (-0.25)
    query_rows = head_major(query_act, heads_here)
    query_scaled = query_rows * scale_in
    key_rows = head_major(key_act, heads_here)
    key_scaled = key_rows * scale_in
    value_matrix = head_major(value_act, heads_here)
    upstream = head_major(grad_out, heads_here)
    query_feature_rows = feature_map(query_rows, omega_seed, query_scaled)
    source_embedding_entries = feature_map(key_rows, omega_seed, key_scaled)
    tok_rows = tokens.shape[0]
    causal = jnp.tril(jnp.ones((tok_rows, tok_rows), jnp.float32))
    block_local_states = ein(
        "vzn,vza->vna", source_embedding_entries, value_matrix
    )
    local_totals = jnp.sum(source_embedding_entries, 1)
    prefix_carried_outer, prefix_normaliser_accrual = carried(
        block_local_states, local_totals, n, 1
    )
    attention_scores = (
        ein(
            "htm,hsm->hts",
            query_feature_rows,
            source_embedding_entries
        )
        * causal
    )
    attention_numerator = ein(
        "xyw,xwc->xyc", attention_scores, value_matrix
    ) + ein(
        "sji,six->sjx", query_feature_rows, prefix_carried_outer
    )
    normer = jnp.sum(attention_scores, -1) + ein(
        "htm,hm->ht", query_feature_rows, prefix_normaliser_accrual
    )
    output = attention_numerator / normer[..., None]
    dividend_cotangent = upstream / normer[..., None]
    normaliser_cotangent = -jnp.sum(upstream * output, -1) / normer
    couplewise_products = (
        ein(
            "htd,hsd->hts", dividend_cotangent, value_matrix
        )
        + normaliser_cotangent[..., None]
    ) * causal
    target_embedding_cotangent = (
        ein(
            "mez,mzo->meo",
            couplewise_products,
            source_embedding_entries
        )
        + ein(
            "zrc,zfc->zrf",
            dividend_cotangent,
            prefix_carried_outer
        )
        + normaliser_cotangent[..., None] * prefix_normaliser_accrual[:, None, :]
    )
    query16 = token_major(
        feature_grad(target_embedding_cotangent, query_feature_rows, query_scaled, omega_seed)
    )
    subsequent_local_states = ein(
        "opu,opc->ouc", query_feature_rows, dividend_cotangent
    )
    later_totals = ein(
        "htm,ht->hm", query_feature_rows, normaliser_cotangent
    )
    subsequent_states, subsequent_sum = carried(
        subsequent_local_states, later_totals, n, -1
    )
    key_feature_gradient = (
        ein(
            "ykl,yku->ylu", couplewise_products, query_feature_rows
        )
        + ein(
            "bgq,bxq->bgx", value_matrix, subsequent_states
        )
        + subsequent_sum[:, None, :]
    )
    value_gradient_rows = ein(
        "vkm,vky->vmy", attention_scores, dividend_cotangent
    ) + ein(
        "tjr,tro->tjo", source_embedding_entries, subsequent_states
    )
    key16 = token_major(
        feature_grad(key_feature_gradient, source_embedding_entries, key_scaled, omega_seed)
    )
    value16 = token_major(value_gradient_rows)
    input_grad, query_wgrad, key_wgrad, value_wgrad = gradients(
        tokens, query16, key16, value16, full, n, groups
    )
    return (input_grad, query_wgrad, key_wgrad, value_wgrad)


def solution(mesh):
    placed = (
        P("seq", None),
        P("seq", "head"),
        P("seq", "head"),
        P("seq", "head"),
        P("head", None, None),
        P("seq", "head"),
    )
    return jax.shard_map(
        functools.partial(per_device, mesh.shape["seq"], mesh.shape["head"]),
        mesh=mesh,
        in_specs=placed,
        out_specs=(P("seq", "head"), P("seq", "head"), P("seq", "head"), P("seq", "head")),
        check_vma=False,
    )
```

```python
import functools
import math

import jax
import jax.numpy as jnp
from jax import lax
from jax.experimental import pallas as pl
from jax.experimental.pallas import tpu as pltpu
from jax.sharding import PartitionSpec as P

seed_step = 0.4
MESH = pl.DeviceIdType.MESH
VMEM = pl.BlockSpec(memory_space=pltpu.VMEM)


def ein(spec, a, b):
    return jnp.einsum(
        spec,
        a.astype(jnp.bfloat16),
        b.astype(jnp.bfloat16),
        preferred_element_type=jnp.float32,
    )


def ring_index(pos, n):
    pos = lax.rem(pos + 2 * n, n)
    odd = lax.div(pos, n // 2)
    return (1 - odd) * (2 * pos) + odd * (2 * (n - 1 - pos) + 1)


def ring_pos(index, n):
    odd = lax.rem(index, 2)
    half = lax.div(index, 2)
    return (1 - odd) * half + odd * (n - 1 - half)


def greet_ring(ahead, behind, others):
    barrier = pltpu.get_barrier_semaphore()
    for device in ({"seq": ahead}, {"seq": behind}):
        pl.semaphore_signal(barrier, inc=1, device_id=device, device_id_type=MESH)
    for device in others:
        pl.semaphore_signal(barrier, inc=1, device_id=device, device_id_type=MESH)
    pl.semaphore_wait(barrier, 2 + len(others))


def pieces_of(rows):
    half = rows // 2
    return tuple((part, pl.ds(part * half, half)) for part in range(2))


def split_columns(cols):
    half = cols // 2
    return (
        (0, slice(0, cols), 0, slice(0, cols)),
        (1, slice(0, half), 0, slice(cols, cols + half)),
        (1, slice(half, cols), 1, slice(0, half)),
        (2, slice(0, cols), 1, slice(half, half + cols)),
    )


def project_kernel(
    n, tok_ref, wq_ref, wk_ref, wv_ref, q_ref, k_ref, v_ref, full_ref, acc, send_sem, recv_sem
):
    me = lax.axis_index("seq")
    place = ring_pos(me, n)
    ahead, behind = ring_index(place + 1, n), ring_index(place - 1, n)
    rows, cols = wq_ref.shape
    greet_ring(ahead, behind, ())
    sources = (wq_ref, wk_ref, wv_ref)
    for matrix, columns, way, target in split_columns(cols):
        full_ref[way, me, :, target] = sources[matrix][:, columns]

    def owner_of(way, step):
        return ring_index(place - step if way == 0 else place + step, n)

    def ring_copy(way, step, part, span):
        owner = owner_of(way, step)
        return pltpu.make_async_remote_copy(
            src_ref=full_ref.at[way, owner, span],
            dst_ref=full_ref.at[way, owner, span],
            send_sem=send_sem.at[way, step, part],
            recv_sem=recv_sem.at[way, step, part],
            device_id={"seq": ahead if way == 0 else behind},
            device_id_type=MESH,
        )

    def arrival(way, step, part, span):
        owner = owner_of(way, step + 1)
        return pltpu.make_async_remote_copy(
            src_ref=full_ref.at[way, owner, span],
            dst_ref=full_ref.at[way, owner, span],
            send_sem=send_sem.at[way, step, part],
            recv_sem=recv_sem.at[way, step, part],
            device_id={"seq": ahead if way == 0 else behind},
            device_id_type=MESH,
        )

    def multiply(step):
        for way in range(2):
            owner = owner_of(way, step)
            columns = pl.ds(pl.multiple_of(owner * rows, rows), rows)
            acc[way] += jnp.dot(
                tok_ref[:, columns], full_ref[way, owner], preferred_element_type=jnp.float32
            )

    for part, span in pieces_of(rows):
        for way in range(2):
            ring_copy(way, 0, part, span).start()
    acc[...] = jnp.zeros_like(acc)
    multiply(0)

    def one(step, carry):
        for part, span in pieces_of(rows):
            for way in range(2):
                arrival(way, step - 1, part, span).wait_recv()
                ring_copy(way, step, part, span).start()
        multiply(step)
        return carry

    lax.fori_loop(1, n - 1, one, 0)
    for part, span in pieces_of(rows):
        for way in range(2):
            arrival(way, n - 2, part, span).wait_recv()
    multiply(n - 1)
    results = (q_ref, k_ref, v_ref)
    for matrix, columns, way, source in split_columns(cols):
        results[matrix][:, columns] = acc[way, :, source].astype(jnp.bfloat16)

    def sent(step, carry):
        for part, span in pieces_of(rows):
            for way in range(2):
                ring_copy(way, step, part, span).wait_send()
        return carry

    lax.fori_loop(0, n - 1, sent, 0)


def project(tokens, w_query, w_key, w_value, n):
    rows, cols = w_query.shape
    width = 3 * cols // 2
    toks = tokens.shape[0]
    act = jax.ShapeDtypeStruct((toks, cols), jnp.bfloat16)
    return pl.pallas_call(
        functools.partial(project_kernel, n),
        out_shape=(act, act, act, jax.ShapeDtypeStruct((2, n, rows, width), jnp.bfloat16)),
        in_specs=[VMEM] * 4,
        out_specs=(VMEM,) * 4,
        scratch_shapes=[
            pltpu.VMEM((2, toks, width), jnp.float32),
            pltpu.SemaphoreType.DMA((2, n - 1, 2)),
            pltpu.SemaphoreType.DMA((2, n - 1, 2)),
        ],
        compiler_params=pltpu.CompilerParams(
            collective_id=0, has_side_effects=True, vmem_limit_bytes=56 << 20
        ),
        cost_estimate=pl.CostEstimate(
            flops=4 * toks * n * rows * width, bytes_accessed=1 << 24, transcendentals=0
        ),
    )(tokens, w_query, w_key, w_value)


PARTS = 4


def scan_kernel(
    n, sign, x_ref, out_ref, pair, pair_out, pair_in, chain_out, chain_in,
    pair_send, pair_recv, chain_send, chain_recv,
):
    me = lax.axis_index("seq")
    odd = lax.rem(me, 2)
    partner = me + 1 - 2 * odd
    half = lax.div(me, 2)
    link = half if sign == 1 else n // 2 - 1 - half
    has_before, has_after = link > 0, link < n // 2 - 1
    before, after = lax.rem(me - 2 * sign + n, n), lax.rem(me + 2 * sign + n, n)
    late = odd if sign == 1 else 1 - odd
    barrier = pltpu.get_barrier_semaphore()
    pl.semaphore_signal(barrier, inc=1, device_id={"seq": partner}, device_id_type=MESH)

    @pl.when(has_before)
    def _():
        pl.semaphore_signal(barrier, inc=1, device_id={"seq": before}, device_id_type=MESH)

    pl.semaphore_wait(barrier, 1 + lax.min(n // 2 - 1 - link, 1))

    size = x_ref.shape[0] // PARTS
    spans = tuple((part, slice(part * size, (part + 1) * size)) for part in range(PARTS))

    def copy(kind, part):
        source, target, send, recv, device = (
            (pair_out, pair_in, pair_send, pair_recv, partner),
            (chain_out, chain_in, chain_send, chain_recv, after),
        )[kind]
        return pltpu.make_async_remote_copy(
            src_ref=source.at[part],
            dst_ref=target.at[part],
            send_sem=send.at[part],
            recv_sem=recv.at[part],
            device_id={"seq": device},
            device_id_type=MESH,
        )

    for part, span in spans:
        pair_out[part] = x_ref[span].astype(jnp.bfloat16)
        copy(0, part).start()
    keep = late.astype(jnp.float32)
    for part, span in spans:
        copy(0, part).wait()
        got = pair_in[part].astype(jnp.float32)
        pair[span] = x_ref[span] + got
        out_ref[span] = got * keep

        @pl.when(has_before)
        def _():
            copy(1, part).wait_recv()
            chained = chain_in[part].astype(jnp.float32)
            out_ref[span] += chained
            pair[span] += chained

        @pl.when(has_after)
        def _():
            chain_out[part] = pair[span].astype(jnp.bfloat16)
            copy(1, part).start()

    @pl.when(has_after)
    def _():
        for part, span in spans:
            copy(1, part).wait_send()


def carried(states, totals, n, sign):
    heads, features, size = states.shape
    split = heads * features
    flat_totals = totals.reshape(-1, size)
    used = flat_totals.shape[0]
    pad = (-(split + used)) % (16 * PARTS)
    packed = jnp.concatenate(
        [states.reshape(-1, size), flat_totals, jnp.zeros((pad, size), jnp.float32)], 0
    )
    piece = (PARTS, packed.shape[0] // PARTS, size)
    out = pl.pallas_call(
        functools.partial(scan_kernel, n, sign),
        out_shape=jax.ShapeDtypeStruct(packed.shape, jnp.float32),
        in_specs=[VMEM],
        out_specs=VMEM,
        scratch_shapes=[
            pltpu.VMEM(packed.shape, jnp.float32),
            *[pltpu.VMEM(piece, jnp.bfloat16)] * 4,
            *[pltpu.SemaphoreType.DMA((PARTS,))] * 4,
        ],
        compiler_params=pltpu.CompilerParams(
            collective_id=1 if sign == 1 else 2,
            has_side_effects=True,
            vmem_limit_bytes=32 << 20,
        ),
    )(packed)
    return out[:split].reshape(states.shape), out[split : split + used].reshape(totals.shape)


def grads_kernel(
    n, groups, tok_ref, q_ref, k_ref, v_ref, full_ref, input_ref, wq_ref, wk_ref, wv_ref,
    grad_ref, ring, own, part_out, part_in, send_sem, recv_sem, part_send, part_recv,
):
    me = lax.axis_index("seq")
    group = lax.axis_index("head")
    place = ring_pos(me, n)
    ahead, behind = ring_index(place + 1, n), ring_index(place - 1, n)
    rows = full_ref.shape[2]
    cols = q_ref.shape[1]
    others = tuple({"head": lax.rem(group + k, groups)} for k in range(1, groups))
    greet_ring(ahead, behind, others)
    sources = (q_ref, k_ref, v_ref)
    for matrix, columns, way, target in split_columns(cols):
        grad_ref[way, :, target] = sources[matrix][:, columns]

    def term(way, step):
        owner = ring_index(place - 1 - step if way == 0 else place + 1 + step, n)
        columns = pl.ds(pl.multiple_of(owner * rows, rows), rows)
        own[way] = lax.dot_general(
            tok_ref[:, columns],
            grad_ref[way],
            (((0,), (0,)), ((), ())),
            preferred_element_type=jnp.float32,
        )

    def ring_copy(way, step, part, span):
        return pltpu.make_async_remote_copy(
            src_ref=ring.at[way, step, span],
            dst_ref=ring.at[way, step + 1, span],
            send_sem=send_sem.at[way, step, part],
            recv_sem=recv_sem.at[way, step, part],
            device_id={"seq": ahead if way == 0 else behind},
            device_id_type=MESH,
        )

    def part_copy(k):
        return pltpu.make_async_remote_copy(
            src_ref=part_out.at[k],
            dst_ref=part_in.at[k],
            send_sem=part_send.at[k],
            recv_sem=part_recv.at[k],
            device_id={"head": lax.rem(group + k + 1, groups)},
            device_id_type=MESH,
        )

    blocks = n // groups

    def one_part(k, carry):
        first = lax.rem(group + k + 1, groups) * blocks

        def one_block(c, carry):
            piece = None
            for way in range(2):
                product = lax.dot_general(
                    grad_ref[way],
                    full_ref[way, first + c],
                    (((1,), (1,)), ((), ())),
                    preferred_element_type=jnp.float32,
                )
                piece = product if piece is None else piece + product
            columns = pl.ds(pl.multiple_of(c * rows, rows), rows)
            part_out[k, :, columns] = piece.astype(jnp.bfloat16)
            return carry

        lax.fori_loop(0, blocks, one_block, 0)

        @pl.when(k < groups - 1)
        def _():
            part_copy(k).start()

        return carry

    for way in range(2):
        term(way, 0)
        for part, span in pieces_of(rows):
            ring[way, 0, span] = own[way, span].astype(jnp.bfloat16)
            ring_copy(way, 0, part, span).start()
    for way in range(2):
        term(way, 1)

    def one(step, carry):
        @pl.when(step <= groups)
        def _():
            one_part(step - 1, 0)

        for part, span in pieces_of(rows):
            for way in range(2):
                ring_copy(way, step - 1, part, span).wait_recv()
                ring[way, step, span] = (
                    ring[way, step, span].astype(jnp.float32) + own[way, span]
                ).astype(jnp.bfloat16)
                ring_copy(way, step, part, span).start()
        for way in range(2):
            term(way, step + 1)
        return carry

    lax.fori_loop(1, n - 1, one, 0)
    if groups > n - 2:
        lax.fori_loop(n - 2, groups, one_part, 0)
    total = part_out[groups - 1].astype(jnp.float32)
    for k in range(groups - 1):
        part_copy(k).wait()
        total += part_in[k].astype(jnp.float32)
    input_ref[...] = total.astype(input_ref.dtype)
    for part, span in pieces_of(rows):
        for way in range(2):
            ring_copy(way, n - 2, part, span).wait_recv()
    results = (wq_ref, wk_ref, wv_ref)
    for matrix, columns, way, source in split_columns(cols):
        results[matrix][:, columns] = (
            ring[way, n - 1, :, source].astype(jnp.float32) + own[way, :, source]
        )

    def sent(step, carry):
        for part, span in pieces_of(rows):
            for way in range(2):
                ring_copy(way, step, part, span).wait_send()
        return carry

    lax.fori_loop(0, n - 1, sent, 0)


def gradients(tokens, query16, key16, value16, full, n, groups):
    ways, _, rows, width = full.shape
    toks, model = tokens.shape
    share = model // groups
    wgrad = jax.ShapeDtypeStruct((rows, query16.shape[1]), jnp.float32)
    return pl.pallas_call(
        functools.partial(grads_kernel, n, groups),
        out_shape=(jax.ShapeDtypeStruct((toks, share), jnp.bfloat16), wgrad, wgrad, wgrad),
        in_specs=[VMEM] * 5,
        out_specs=(VMEM,) * 4,
        scratch_shapes=[
            pltpu.VMEM((ways, toks, width), jnp.bfloat16),
            pltpu.VMEM((ways, n, rows, width), jnp.bfloat16),
            pltpu.VMEM((ways, rows, width), jnp.float32),
            pltpu.VMEM((groups, toks, share), jnp.bfloat16),
            pltpu.VMEM((groups - 1, toks, share), jnp.bfloat16),
            pltpu.SemaphoreType.DMA((2, n - 1, 2)),
            pltpu.SemaphoreType.DMA((2, n - 1, 2)),
            pltpu.SemaphoreType.DMA((groups - 1,)),
            pltpu.SemaphoreType.DMA((groups - 1,)),
        ],
        compiler_params=pltpu.CompilerParams(
            collective_id=3, has_side_effects=True, vmem_limit_bytes=60 << 20
        ),
    )(tokens, query16, key16, value16, full)


def feature_map(act, seed, scaled):
    factor = seed_step * act.shape[-1] ** (-0.25)
    projected = ein("htd,hdm->htm", act, seed) * factor
    return jnp.exp(projected - 0.5 * jnp.sum(scaled * scaled, -1, keepdims=True)) / math.sqrt(
        seed.shape[-1]
    )


def feature_grad(upstream, features, scaled, seed):
    weighted = upstream * features
    projected = ein("htm,hdm->htd", weighted, seed) * seed_step
    return (projected - jnp.sum(weighted, -1, keepdims=True) * scaled) * scaled.shape[-1] ** (-0.25)


def head_major(value_matrix, heads_here):
    tok_rows = value_matrix.shape[0]
    return value_matrix.astype(jnp.float32).reshape(tok_rows, heads_here, -1).transpose(1, 0, 2)


def token_major(value_matrix):
    return value_matrix.transpose(1, 0, 2).reshape(value_matrix.shape[1], -1).astype(jnp.bfloat16)


def per_device(n, groups, tokens, w_query, w_key, w_value, omega_seed, grad_out):
    heads_here = omega_seed.shape[0]
    head_size = omega_seed.shape[1]
    query_act, key_act, value_act, full = project(tokens, w_query, w_key, w_value, n)
    scale_in = head_size ** (-0.25)
    query_rows = head_major(query_act, heads_here)
    query_scaled = query_rows * scale_in
    key_rows = head_major(key_act, heads_here)
    key_scaled = key_rows * scale_in
    value_matrix = head_major(value_act, heads_here)
    upstream = head_major(grad_out, heads_here)
    query_feature_rows = feature_map(query_rows, omega_seed, query_scaled)
    source_embedding_entries = feature_map(key_rows, omega_seed, key_scaled)
    tok_rows = tokens.shape[0]
    causal = jnp.tril(jnp.ones((tok_rows, tok_rows), jnp.float32))
    block_local_states = ein(
        "vzn,vza->vna", source_embedding_entries, value_matrix
    )
    local_totals = jnp.sum(source_embedding_entries, 1)
    prefix_carried_outer, prefix_normaliser_accrual = carried(
        block_local_states, local_totals, n, 1
    )
    attention_scores = (
        ein(
            "htm,hsm->hts",
            query_feature_rows,
            source_embedding_entries
        )
        * causal
    )
    attention_numerator = ein(
        "xyw,xwc->xyc", attention_scores, value_matrix
    ) + ein(
        "sji,six->sjx", query_feature_rows, prefix_carried_outer
    )
    normer = jnp.sum(attention_scores, -1) + ein(
        "htm,hm->ht", query_feature_rows, prefix_normaliser_accrual
    )
    output = attention_numerator / normer[..., None]
    dividend_cotangent = upstream / normer[..., None]
    normaliser_cotangent = -jnp.sum(upstream * output, -1) / normer
    couplewise_products = (
        ein(
            "htd,hsd->hts", dividend_cotangent, value_matrix
        )
        + normaliser_cotangent[..., None]
    ) * causal
    target_embedding_cotangent = (
        ein(
            "mez,mzo->meo",
            couplewise_products,
            source_embedding_entries
        )
        + ein(
            "zrc,zfc->zrf",
            dividend_cotangent,
            prefix_carried_outer
        )
        + normaliser_cotangent[..., None] * prefix_normaliser_accrual[:, None, :]
    )
    query16 = token_major(
        feature_grad(target_embedding_cotangent, query_feature_rows, query_scaled, omega_seed)
    )
    subsequent_local_states = ein(
        "opu,opc->ouc", query_feature_rows, dividend_cotangent
    )
    later_totals = ein(
        "htm,ht->hm", query_feature_rows, normaliser_cotangent
    )
    subsequent_states, subsequent_sum = carried(
        subsequent_local_states, later_totals, n, -1
    )
    key_feature_gradient = (
        ein(
            "ykl,yku->ylu", couplewise_products, query_feature_rows
        )
        + ein(
            "bgq,bxq->bgx", value_matrix, subsequent_states
        )
        + subsequent_sum[:, None, :]
    )
    value_gradient_rows = ein(
        "vkm,vky->vmy", attention_scores, dividend_cotangent
    ) + ein(
        "tjr,tro->tjo", source_embedding_entries, subsequent_states
    )
    key16 = token_major(
        feature_grad(key_feature_gradient, source_embedding_entries, key_scaled, omega_seed)
    )
    value16 = token_major(value_gradient_rows)
    input_grad, query_wgrad, key_wgrad, value_wgrad = gradients(
        tokens, query16, key16, value16, full, n, groups
    )
    return (input_grad, query_wgrad, key_wgrad, value_wgrad)


def solution(mesh):
    placed = (
        P("seq", None),
        P("seq", "head"),
        P("seq", "head"),
        P("seq", "head"),
        P("head", None, None),
        P("seq", "head"),
    )
    return jax.shard_map(
        functools.partial(per_device, mesh.shape["seq"], mesh.shape["head"]),
        mesh=mesh,
        in_specs=placed,
        out_specs=(P("seq", "head"), P("seq", "head"), P("seq", "head"), P("seq", "head")),
        check_vma=False,
    )
```

```python
import functools
import math

import jax
import jax.numpy as jnp
from jax import lax
from jax.experimental import pallas as pl
from jax.experimental.pallas import tpu as pltpu
from jax.sharding import PartitionSpec as P

seed_step = 0.4
MESH = pl.DeviceIdType.MESH
VMEM = pl.BlockSpec(memory_space=pltpu.VMEM)


def ein(spec, a, b):
    return jnp.einsum(
        spec,
        a.astype(jnp.bfloat16),
        b.astype(jnp.bfloat16),
        preferred_element_type=jnp.float32,
    )


def ring_index(pos, n):
    pos = lax.rem(pos + 2 * n, n)
    odd = lax.div(pos, n // 2)
    return (1 - odd) * (2 * pos) + odd * (2 * (n - 1 - pos) + 1)


def ring_pos(index, n):
    odd = lax.rem(index, 2)
    half = lax.div(index, 2)
    return (1 - odd) * half + odd * (n - 1 - half)


def greet_ring(ahead, behind, others):
    barrier = pltpu.get_barrier_semaphore()
    for device in ({"seq": ahead}, {"seq": behind}):
        pl.semaphore_signal(barrier, inc=1, device_id=device, device_id_type=MESH)
    for device in others:
        pl.semaphore_signal(barrier, inc=1, device_id=device, device_id_type=MESH)
    pl.semaphore_wait(barrier, 2 + len(others))


def pieces_of(rows):
    half = rows // 2
    return tuple((part, pl.ds(part * half, half)) for part in range(2))


def split_columns(cols):
    half = cols // 2
    return (
        (0, slice(0, cols), 0, slice(0, cols)),
        (1, slice(0, half), 0, slice(cols, cols + half)),
        (1, slice(half, cols), 1, slice(0, half)),
        (2, slice(0, cols), 1, slice(half, half + cols)),
    )


def project_kernel(
    n, tok_ref, wq_ref, wk_ref, wv_ref, q_ref, k_ref, v_ref, full_ref, acc, send_sem, recv_sem
):
    me = lax.axis_index("seq")
    place = ring_pos(me, n)
    ahead, behind = ring_index(place + 1, n), ring_index(place - 1, n)
    rows, cols = wq_ref.shape
    greet_ring(ahead, behind, ())
    sources = (wq_ref, wk_ref, wv_ref)
    for matrix, columns, way, target in split_columns(cols):
        full_ref[way, me, :, target] = sources[matrix][:, columns]

    def owner_of(way, step):
        return ring_index(place - step if way == 0 else place + step, n)

    def ring_copy(way, step, part, span):
        owner = owner_of(way, step)
        return pltpu.make_async_remote_copy(
            src_ref=full_ref.at[way, owner, span],
            dst_ref=full_ref.at[way, owner, span],
            send_sem=send_sem.at[way, step, part],
            recv_sem=recv_sem.at[way, step, part],
            device_id={"seq": ahead if way == 0 else behind},
            device_id_type=MESH,
        )

    def arrival(way, step, part, span):
        owner = owner_of(way, step + 1)
        return pltpu.make_async_remote_copy(
            src_ref=full_ref.at[way, owner, span],
            dst_ref=full_ref.at[way, owner, span],
            send_sem=send_sem.at[way, step, part],
            recv_sem=recv_sem.at[way, step, part],
            device_id={"seq": ahead if way == 0 else behind},
            device_id_type=MESH,
        )

    def multiply(step):
        for way in range(2):
            owner = owner_of(way, step)
            columns = pl.ds(pl.multiple_of(owner * rows, rows), rows)
            acc[way] += jnp.dot(
                tok_ref[:, columns], full_ref[way, owner], preferred_element_type=jnp.float32
            )

    for part, span in pieces_of(rows):
        for way in range(2):
            ring_copy(way, 0, part, span).start()
    acc[...] = jnp.zeros_like(acc)
    multiply(0)

    def one(step, carry):
        for part, span in pieces_of(rows):
            for way in range(2):
                arrival(way, step - 1, part, span).wait_recv()
                ring_copy(way, step, part, span).start()
        multiply(step)
        return carry

    lax.fori_loop(1, n - 1, one, 0)
    for part, span in pieces_of(rows):
        for way in range(2):
            arrival(way, n - 2, part, span).wait_recv()
    multiply(n - 1)
    results = (q_ref, k_ref, v_ref)
    for matrix, columns, way, source in split_columns(cols):
        results[matrix][:, columns] = acc[way, :, source].astype(jnp.bfloat16)

    def sent(step, carry):
        for part, span in pieces_of(rows):
            for way in range(2):
                ring_copy(way, step, part, span).wait_send()
        return carry

    lax.fori_loop(0, n - 1, sent, 0)


def project(tokens, w_query, w_key, w_value, n):
    rows, cols = w_query.shape
    width = 3 * cols // 2
    toks = tokens.shape[0]
    act = jax.ShapeDtypeStruct((toks, cols), jnp.bfloat16)
    return pl.pallas_call(
        functools.partial(project_kernel, n),
        out_shape=(act, act, act, jax.ShapeDtypeStruct((2, n, rows, width), jnp.bfloat16)),
        in_specs=[VMEM] * 4,
        out_specs=(VMEM,) * 4,
        scratch_shapes=[
            pltpu.VMEM((2, toks, width), jnp.float32),
            pltpu.SemaphoreType.DMA((2, n - 1, 2)),
            pltpu.SemaphoreType.DMA((2, n - 1, 2)),
        ],
        compiler_params=pltpu.CompilerParams(
            collective_id=0, has_side_effects=True, vmem_limit_bytes=56 << 20
        ),
        cost_estimate=pl.CostEstimate(
            flops=4 * toks * n * rows * width, bytes_accessed=1 << 24, transcendentals=0
        ),
    )(tokens, w_query, w_key, w_value)


PARTS = 8


def scan_kernel(
    n, sign, x_ref, out_ref, pair, pair_out, pair_in, chain_out, chain_in,
    pair_send, pair_recv, chain_send, chain_recv,
):
    me = lax.axis_index("seq")
    odd = lax.rem(me, 2)
    partner = me + 1 - 2 * odd
    half = lax.div(me, 2)
    link = half if sign == 1 else n // 2 - 1 - half
    has_before, has_after = link > 0, link < n // 2 - 1
    before, after = lax.rem(me - 2 * sign + n, n), lax.rem(me + 2 * sign + n, n)
    late = odd if sign == 1 else 1 - odd
    barrier = pltpu.get_barrier_semaphore()
    pl.semaphore_signal(barrier, inc=1, device_id={"seq": partner}, device_id_type=MESH)

    @pl.when(has_before)
    def _():
        pl.semaphore_signal(barrier, inc=1, device_id={"seq": before}, device_id_type=MESH)

    pl.semaphore_wait(barrier, 1 + lax.min(n // 2 - 1 - link, 1))

    size = x_ref.shape[0] // PARTS
    spans = tuple((part, slice(part * size, (part + 1) * size)) for part in range(PARTS))

    def copy(kind, part):
        source, target, send, recv, device = (
            (pair_out, pair_in, pair_send, pair_recv, partner),
            (chain_out, chain_in, chain_send, chain_recv, after),
        )[kind]
        return pltpu.make_async_remote_copy(
            src_ref=source.at[part],
            dst_ref=target.at[part],
            send_sem=send.at[part],
            recv_sem=recv.at[part],
            device_id={"seq": device},
            device_id_type=MESH,
        )

    for part, span in spans:
        pair_out[part] = x_ref[span].astype(jnp.bfloat16)
        copy(0, part).start()
    keep = late.astype(jnp.float32)
    for part, span in spans:
        copy(0, part).wait()
        got = pair_in[part].astype(jnp.float32)
        pair[span] = x_ref[span] + got
        out_ref[span] = got * keep

        @pl.when(has_before)
        def _():
            copy(1, part).wait_recv()
            chained = chain_in[part].astype(jnp.float32)
            out_ref[span] += chained
            pair[span] += chained

        @pl.when(has_after)
        def _():
            chain_out[part] = pair[span].astype(jnp.bfloat16)
            copy(1, part).start()

    @pl.when(has_after)
    def _():
        for part, span in spans:
            copy(1, part).wait_send()


def carried(states, totals, n, sign):
    heads, features, size = states.shape
    split = heads * features
    flat_totals = totals.reshape(-1, size)
    used = flat_totals.shape[0]
    pad = (-(split + used)) % (16 * PARTS)
    packed = jnp.concatenate(
        [states.reshape(-1, size), flat_totals, jnp.zeros((pad, size), jnp.float32)], 0
    )
    piece = (PARTS, packed.shape[0] // PARTS, size)
    out = pl.pallas_call(
        functools.partial(scan_kernel, n, sign),
        out_shape=jax.ShapeDtypeStruct(packed.shape, jnp.float32),
        in_specs=[VMEM],
        out_specs=VMEM,
        scratch_shapes=[
            pltpu.VMEM(packed.shape, jnp.float32),
            *[pltpu.VMEM(piece, jnp.bfloat16)] * 4,
            *[pltpu.SemaphoreType.DMA((PARTS,))] * 4,
        ],
        compiler_params=pltpu.CompilerParams(
            collective_id=1 if sign == 1 else 2,
            has_side_effects=True,
            vmem_limit_bytes=32 << 20,
        ),
    )(packed)
    return out[:split].reshape(states.shape), out[split : split + used].reshape(totals.shape)


def grads_kernel(
    n, groups, tok_ref, q_ref, k_ref, v_ref, full_ref, input_ref, wq_ref, wk_ref, wv_ref,
    grad_ref, ring, own, part_out, part_in, send_sem, recv_sem, part_send, part_recv,
):
    me = lax.axis_index("seq")
    group = lax.axis_index("head")
    place = ring_pos(me, n)
    ahead, behind = ring_index(place + 1, n), ring_index(place - 1, n)
    rows = full_ref.shape[2]
    cols = q_ref.shape[1]
    others = tuple({"head": lax.rem(group + k, groups)} for k in range(1, groups))
    greet_ring(ahead, behind, others)
    sources = (q_ref, k_ref, v_ref)
    for matrix, columns, way, target in split_columns(cols):
        grad_ref[way, :, target] = sources[matrix][:, columns]

    def term(way, step):
        owner = ring_index(place - 1 - step if way == 0 else place + 1 + step, n)
        columns = pl.ds(pl.multiple_of(owner * rows, rows), rows)
        own[way] = lax.dot_general(
            tok_ref[:, columns],
            grad_ref[way],
            (((0,), (0,)), ((), ())),
            preferred_element_type=jnp.float32,
        )

    def ring_copy(way, step, part, span):
        return pltpu.make_async_remote_copy(
            src_ref=ring.at[way, step, span],
            dst_ref=ring.at[way, step + 1, span],
            send_sem=send_sem.at[way, step, part],
            recv_sem=recv_sem.at[way, step, part],
            device_id={"seq": ahead if way == 0 else behind},
            device_id_type=MESH,
        )

    def part_copy(k):
        return pltpu.make_async_remote_copy(
            src_ref=part_out.at[k],
            dst_ref=part_in.at[k],
            send_sem=part_send.at[k],
            recv_sem=part_recv.at[k],
            device_id={"head": lax.rem(group + k + 1, groups)},
            device_id_type=MESH,
        )

    blocks = n // groups

    def one_part(k, carry):
        first = lax.rem(group + k + 1, groups) * blocks

        def one_block(c, carry):
            piece = None
            for way in range(2):
                product = lax.dot_general(
                    grad_ref[way],
                    full_ref[way, first + c],
                    (((1,), (1,)), ((), ())),
                    preferred_element_type=jnp.float32,
                )
                piece = product if piece is None else piece + product
            columns = pl.ds(pl.multiple_of(c * rows, rows), rows)
            part_out[k, :, columns] = piece.astype(jnp.bfloat16)
            return carry

        lax.fori_loop(0, blocks, one_block, 0)

        @pl.when(k < groups - 1)
        def _():
            part_copy(k).start()

        return carry

    for way in range(2):
        term(way, 0)
        for part, span in pieces_of(rows):
            ring[way, 0, span] = own[way, span].astype(jnp.bfloat16)
            ring_copy(way, 0, part, span).start()
    for way in range(2):
        term(way, 1)

    def one(step, carry):
        @pl.when(step <= groups)
        def _():
            one_part(step - 1, 0)

        for part, span in pieces_of(rows):
            for way in range(2):
                ring_copy(way, step - 1, part, span).wait_recv()
                ring[way, step, span] = (
                    ring[way, step, span].astype(jnp.float32) + own[way, span]
                ).astype(jnp.bfloat16)
                ring_copy(way, step, part, span).start()
        for way in range(2):
            term(way, step + 1)
        return carry

    lax.fori_loop(1, n - 1, one, 0)
    if groups > n - 2:
        lax.fori_loop(n - 2, groups, one_part, 0)
    total = part_out[groups - 1].astype(jnp.float32)
    for k in range(groups - 1):
        part_copy(k).wait()
        total += part_in[k].astype(jnp.float32)
    input_ref[...] = total.astype(input_ref.dtype)
    for part, span in pieces_of(rows):
        for way in range(2):
            ring_copy(way, n - 2, part, span).wait_recv()
    results = (wq_ref, wk_ref, wv_ref)
    for matrix, columns, way, source in split_columns(cols):
        results[matrix][:, columns] = (
            ring[way, n - 1, :, source].astype(jnp.float32) + own[way, :, source]
        )

    def sent(step, carry):
        for part, span in pieces_of(rows):
            for way in range(2):
                ring_copy(way, step, part, span).wait_send()
        return carry

    lax.fori_loop(0, n - 1, sent, 0)


def gradients(tokens, query16, key16, value16, full, n, groups):
    ways, _, rows, width = full.shape
    toks, model = tokens.shape
    share = model // groups
    wgrad = jax.ShapeDtypeStruct((rows, query16.shape[1]), jnp.float32)
    return pl.pallas_call(
        functools.partial(grads_kernel, n, groups),
        out_shape=(jax.ShapeDtypeStruct((toks, share), jnp.bfloat16), wgrad, wgrad, wgrad),
        in_specs=[VMEM] * 5,
        out_specs=(VMEM,) * 4,
        scratch_shapes=[
            pltpu.VMEM((ways, toks, width), jnp.bfloat16),
            pltpu.VMEM((ways, n, rows, width), jnp.bfloat16),
            pltpu.VMEM((ways, rows, width), jnp.float32),
            pltpu.VMEM((groups, toks, share), jnp.bfloat16),
            pltpu.VMEM((groups - 1, toks, share), jnp.bfloat16),
            pltpu.SemaphoreType.DMA((2, n - 1, 2)),
            pltpu.SemaphoreType.DMA((2, n - 1, 2)),
            pltpu.SemaphoreType.DMA((groups - 1,)),
            pltpu.SemaphoreType.DMA((groups - 1,)),
        ],
        compiler_params=pltpu.CompilerParams(
            collective_id=3, has_side_effects=True, vmem_limit_bytes=60 << 20
        ),
    )(tokens, query16, key16, value16, full)


def feature_map(act, seed, scaled):
    factor = seed_step * act.shape[-1] ** (-0.25)
    projected = ein("htd,hdm->htm", act, seed) * factor
    return jnp.exp(projected - 0.5 * jnp.sum(scaled * scaled, -1, keepdims=True)) / math.sqrt(
        seed.shape[-1]
    )


def feature_grad(upstream, features, scaled, seed):
    weighted = upstream * features
    projected = ein("htm,hdm->htd", weighted, seed) * seed_step
    return (projected - jnp.sum(weighted, -1, keepdims=True) * scaled) * scaled.shape[-1] ** (-0.25)


def head_major(value_matrix, heads_here):
    tok_rows = value_matrix.shape[0]
    return value_matrix.astype(jnp.float32).reshape(tok_rows, heads_here, -1).transpose(1, 0, 2)


def token_major(value_matrix):
    return value_matrix.transpose(1, 0, 2).reshape(value_matrix.shape[1], -1).astype(jnp.bfloat16)


def per_device(n, groups, tokens, w_query, w_key, w_value, omega_seed, grad_out):
    heads_here = omega_seed.shape[0]
    head_size = omega_seed.shape[1]
    query_act, key_act, value_act, full = project(tokens, w_query, w_key, w_value, n)
    scale_in = head_size ** (-0.25)
    query_rows = head_major(query_act, heads_here)
    query_scaled = query_rows * scale_in
    key_rows = head_major(key_act, heads_here)
    key_scaled = key_rows * scale_in
    value_matrix = head_major(value_act, heads_here)
    upstream = head_major(grad_out, heads_here)
    query_feature_rows = feature_map(query_rows, omega_seed, query_scaled)
    source_embedding_entries = feature_map(key_rows, omega_seed, key_scaled)
    tok_rows = tokens.shape[0]
    causal = jnp.tril(jnp.ones((tok_rows, tok_rows), jnp.float32))
    block_local_states = ein(
        "vzn,vza->vna", source_embedding_entries, value_matrix
    )
    local_totals = jnp.sum(source_embedding_entries, 1)
    prefix_carried_outer, prefix_normaliser_accrual = carried(
        block_local_states, local_totals, n, 1
    )
    attention_scores = (
        ein(
            "htm,hsm->hts",
            query_feature_rows,
            source_embedding_entries
        )
        * causal
    )
    attention_numerator = ein(
        "xyw,xwc->xyc", attention_scores, value_matrix
    ) + ein(
        "sji,six->sjx", query_feature_rows, prefix_carried_outer
    )
    normer = jnp.sum(attention_scores, -1) + ein(
        "htm,hm->ht", query_feature_rows, prefix_normaliser_accrual
    )
    output = attention_numerator / normer[..., None]
    dividend_cotangent = upstream / normer[..., None]
    normaliser_cotangent = -jnp.sum(upstream * output, -1) / normer
    couplewise_products = (
        ein(
            "htd,hsd->hts", dividend_cotangent, value_matrix
        )
        + normaliser_cotangent[..., None]
    ) * causal
    target_embedding_cotangent = (
        ein(
            "mez,mzo->meo",
            couplewise_products,
            source_embedding_entries
        )
        + ein(
            "zrc,zfc->zrf",
            dividend_cotangent,
            prefix_carried_outer
        )
        + normaliser_cotangent[..., None] * prefix_normaliser_accrual[:, None, :]
    )
    query16 = token_major(
        feature_grad(target_embedding_cotangent, query_feature_rows, query_scaled, omega_seed)
    )
    subsequent_local_states = ein(
        "opu,opc->ouc", query_feature_rows, dividend_cotangent
    )
    later_totals = ein(
        "htm,ht->hm", query_feature_rows, normaliser_cotangent
    )
    subsequent_states, subsequent_sum = carried(
        subsequent_local_states, later_totals, n, -1
    )
    key_feature_gradient = (
        ein(
            "ykl,yku->ylu", couplewise_products, query_feature_rows
        )
        + ein(
            "bgq,bxq->bgx", value_matrix, subsequent_states
        )
        + subsequent_sum[:, None, :]
    )
    value_gradient_rows = ein(
        "vkm,vky->vmy", attention_scores, dividend_cotangent
    ) + ein(
        "tjr,tro->tjo", source_embedding_entries, subsequent_states
    )
    key16 = token_major(
        feature_grad(key_feature_gradient, source_embedding_entries, key_scaled, omega_seed)
    )
    value16 = token_major(value_gradient_rows)
    input_grad, query_wgrad, key_wgrad, value_wgrad = gradients(
        tokens, query16, key16, value16, full, n, groups
    )
    return (input_grad, query_wgrad, key_wgrad, value_wgrad)


def solution(mesh):
    placed = (
        P("seq", None),
        P("seq", "head"),
        P("seq", "head"),
        P("seq", "head"),
        P("head", None, None),
        P("seq", "head"),
    )
    return jax.shard_map(
        functools.partial(per_device, mesh.shape["seq"], mesh.shape["head"]),
        mesh=mesh,
        in_specs=placed,
        out_specs=(P("seq", "head"), P("seq", "head"), P("seq", "head"), P("seq", "head")),
        check_vma=False,
    )
```
